1024 devices in a mesh: row: 16 (over x, y), depth: 64 (over z, core).
Axes of the slice: x: 4, y: 4, z: 32, core: 2. Of those that a mesh axis runs over, the one named last changes fastest.
Arguments:
- integrals: bfloat16 [45056, 40960], P('row', 'depth'), may hold values from -0.02734375 to 0.02734375
- amplitudes: bfloat16 [45056, 200], P(('row', 'depth')), may hold values from -6 to 6
Outputs:
- ladder: bfloat16 [40960, 200], P('depth')
The draws below stay inside these ranges and needn't reach their ends.
All inputs are finite; a program needn't handle non-finite values.
Results may differ from the reference program's by a relative error of at most 0.001.
Values may be sent and summed in bfloat16 or wider, within the bound.
No kernel may reach another device: no remote copies, remote signals or barrier semaphores. Data moves between devices by JAX's collectives and lax.ppermute only.
A program may use at most 32 MiB of HBM per device.

```python
import math
import jax
import jax.numpy as jnp
from jax import lax

OO = 200
K = 45056
AB = 40960


def shard_levels(stream_key, shape, cuts, smallest, largest):
    def one(position, shards_of):
        draws = jax.random.uniform(jax.random.fold_in(jax.random.fold_in(stream_key, 6), position), (shards_of,), jnp.float32, smallest / len(cuts), largest / len(cuts))
        return jnp.repeat(jnp.exp(draws), shape[position] // shards_of).reshape((-1,) + (1,) * (len(shape) - position - 1))

    gain = one(*cuts[0])
    for cut in cuts[1:]:
        gain = gain * one(*cut)
    return gain


def gaussian(stream_key, dims, spread, most, pieces=(), held_as=jnp.bfloat16):
    entries = jax.random.normal(stream_key, dims, jnp.float32) * spread
    if len(pieces) > 0:
        entries = shard_levels(stream_key, dims, pieces, -0.22, 0.18) * entries
    return jnp.clip(entries, min=-most, max=most).astype(held_as)


def setup_inputs(seed: int = 0) -> dict:
    seeds = jax.random.split(jax.random.key(seed), 3)
    integrals = gaussian(seeds[0], (K, AB), K ** -0.5, 0.02734375, ((0, 16), (1, 64)))
    amplitudes = gaussian(seeds[1], (K, OO), 1.0, 6.0, ((0, 1024),))
    return {"integrals": integrals, "amplitudes": amplitudes}


def reference(integrals, amplitudes):
    width = math.gcd(AB, 1024)

    def column_block(index):
        columns = lax.dynamic_slice_in_dim(integrals, (index * width).astype(jnp.int32), width, 1)
        return lax.dot_general(columns, amplitudes, (((0,), (0,)), ((), ())), preferred_element_type=jnp.float32).astype(jnp.bfloat16)

    blocks = lax.map(column_block, jnp.arange(AB // width, dtype=jnp.int32))
    return blocks.reshape(AB, OO)
```

```python
import jax
import jax.numpy as jnp
from jax import lax
from jax.experimental import pallas as pl
from jax.experimental.pallas import tpu as pltpu
from jax.sharding import PartitionSpec as P

CUBE = 4
CORES = 2
LANES = 128
MIB = 1 << 20


def depth_groups(depth):
    cubes = depth // (CUBE * CORES)
    across = [
        [(b * CUBE + i) * CORES + c for b in range(cubes)]
        for i in range(CUBE)
        for c in range(CORES)
    ]
    inside = [
        [(b * CUBE + i) * CORES + c for i in range(CUBE)]
        for b in range(cubes)
        for c in range(CORES)
    ]
    return cubes, across, inside


def contract_kernel(core_ref, mine_ref, other_ref, integrals_hbm, out_ref, integrals, lines, turned, sem):
    chips, cubes, rows, ij = mine_ref.shape
    fetch = pltpu.make_async_copy(integrals_hbm, integrals, sem)
    fetch.start()
    first = core_ref[0] == 0
    for b in range(cubes):
        for i in range(chips):
            mine = mine_ref[i, b].astype(jnp.float32)
            other = other_ref[i, b].astype(jnp.float32)
            at = (b * chips + i) * CORES * rows
            lines[at : at + rows, :] = jnp.where(first, mine, other)
            lines[at + rows : at + 2 * rows, :] = jnp.where(first, other, mine)
    depth = lines.shape[0]
    for k in range(0, depth, 256):
        turned[:, k : k + 256] = lines[k : k + 256, :].T.astype(jnp.bfloat16)
    fetch.wait()
    for n in range(integrals.shape[1] // LANES):
        out_ref[n * ij : (n + 1) * ij, :] = jnp.dot(
            turned[...],
            integrals[:, n * LANES : (n + 1) * LANES],
            preferred_element_type=jnp.float32,
        )
    used = integrals.shape[1] // LANES * ij
    out_ref[used:, :] = jnp.zeros((out_ref.shape[0] - used, LANES), jnp.float32)


def contract(core, mine, other, integrals, lines_out):
    k, ab = integrals.shape
    ij = mine.shape[-1]
    vmem = pl.BlockSpec(memory_space=pltpu.VMEM)
    return pl.pallas_call(
        contract_kernel,
        out_shape=jax.ShapeDtypeStruct((lines_out, LANES), jnp.float32),
        in_specs=[
            pl.BlockSpec(memory_space=pltpu.SMEM),
            vmem,
            vmem,
            pl.BlockSpec(memory_space=pl.ANY),
        ],
        out_specs=vmem,
        scratch_shapes=[
            pltpu.VMEM((k, ab), jnp.bfloat16),
            pltpu.VMEM((k, ij), jnp.float32),
            pltpu.VMEM((ij, k), jnp.bfloat16),
            pltpu.SemaphoreType.DMA,
        ],
        compiler_params=pltpu.CompilerParams(vmem_limit_bytes=32 * MIB),
        cost_estimate=pl.CostEstimate(
            flops=2 * k * ab * ij, bytes_accessed=2 * k * (ab + ij), transcendentals=0
        ),
        name="contract",
    )(core, mine, other, integrals)


def total_kernel(terms_ref, out_ref):
    total = terms_ref[0]
    for r in range(1, terms_ref.shape[0]):
        total = total + terms_ref[r]
    total = total.astype(jnp.bfloat16)
    for r in range(out_ref.shape[0]):
        out_ref[r] = total


def totals(terms):
    vmem = pl.BlockSpec(memory_space=pltpu.VMEM)
    return pl.pallas_call(
        total_kernel,
        out_shape=jax.ShapeDtypeStruct(terms.shape, jnp.bfloat16),
        in_specs=[vmem],
        out_specs=vmem,
        name="totals",
    )(terms)


def order_kernel(lines_ref, out_ref):
    ij, ab = out_ref.shape
    for n in range(ab // LANES):
        out_ref[:, n * LANES : (n + 1) * LANES] = (
            lines_ref[n * ij : (n + 1) * ij, :]
            .astype(jnp.float32)
            .astype(jnp.bfloat16)
        )


def ordered(lines, ij, ab):
    vmem = pl.BlockSpec(memory_space=pltpu.VMEM)
    return pl.pallas_call(
        order_kernel,
        out_shape=jax.ShapeDtypeStruct((ij, ab), jnp.bfloat16),
        in_specs=[vmem],
        out_specs=vmem,
        name="ordered",
    )(lines)


def solution(mesh):
    rows, depth = mesh.shape["row"], mesh.shape["depth"]
    cubes, across, inside = depth_groups(depth)

    def shards(integrals, amplitudes):
        ij, ab = amplitudes.shape[1], integrals.shape[1]
        copies = jnp.broadcast_to(amplitudes[None], (cubes, *amplitudes.shape))
        mine = lax.all_to_all(copies, "depth", 0, 0, axis_index_groups=across)
        mine = lax.all_gather(mine, "depth", axis_index_groups=inside)
        other = lax.ppermute(mine, "depth", [(d, d ^ 1) for d in range(depth)])
        core = lax.rem(lax.axis_index("depth"), CORES).reshape(1)

        share = -(-ij * ab // (LANES * rows * 16)) * 16
        partial = contract(core, mine, other, integrals, rows * share)
        terms = lax.all_to_all(partial.reshape(rows, share, LANES), "row", 0, 0)
        whole = lax.all_to_all(totals(terms), "row", 0, 0)
        return ordered(whole.reshape(rows * share, LANES), ij, ab).T

    placed = (P("row", "depth"), P(("row", "depth"), None))
    return jax.shard_map(
        shards, mesh=mesh, in_specs=placed, out_specs=P("depth", None), check_vma=False
    )
```

```python
import jax
import jax.numpy as jnp
from jax import lax
from jax.experimental import pallas as pl
from jax.experimental.pallas import tpu as pltpu
from jax.sharding import PartitionSpec as P

CUBE = 4
CORES = 2
LANES = 128
MIB = 1 << 20


def depth_groups(depth):
    cubes = depth // (CUBE * CORES)
    inside = [
        [(b * CUBE + i) * CORES + c for i in range(CUBE)]
        for b in range(cubes)
        for c in range(CORES)
    ]
    chips = [[d, d + 1] for d in range(0, depth, CORES)]
    return cubes, inside, chips


def hop(depth, cubes):
    step = cubes * CUBE * CORES
    return [(d, (d + step * (1 - 2 * (d % CORES))) % depth) for d in range(depth)]


def spread(amplitudes, depth):
    cubes, _, chips = depth_groups(depth)
    pair = lax.all_gather(amplitudes, "depth", axis_index_groups=chips)
    opposite = lax.ppermute(amplitudes, "depth", hop(depth, cubes // 2))
    pairs = [
        lax.ppermute(pair, "depth", hop(depth, k))
        for k in range(cubes // 2 - 1, 0, -1)
    ]
    return jnp.concatenate([amplitudes[None], opposite[None], *pairs], axis=0)


def contract_kernel(
    place_ref, mine_ref, other_ref, integrals_hbm, out_ref, integrals, lines, turned, sem
):
    chips, cubes, rows, ij = mine_ref.shape
    fetch = pltpu.make_async_copy(integrals_hbm, integrals, sem)
    fetch.start()
    cube, core = place_ref[0], place_ref[1]
    first = core == 0
    up = 1 - 2 * core

    def put(b, i, upper, lower):
        at = pl.multiple_of((b * chips + i) * (CORES * rows), 8)
        lines[pl.ds(at, CORES * rows), :] = jnp.concatenate([upper, lower], axis=0)

    def load(ref, i, j):
        return ref[i, j].astype(jnp.float32)

    for i in range(chips):
        for j, away in ((0, 0), (1, cubes // 2)):
            mine, other = load(mine_ref, i, j), load(other_ref, i, j)
            upper, lower = jnp.where(first, mine, other), jnp.where(first, other, mine)
            put(lax.rem(cube + away, cubes), i, upper, lower)
        for j, k in enumerate(range(cubes // 2 - 1, 0, -1)):
            for ref, sign in ((mine_ref, -up), (other_ref, up)):
                b = lax.rem(cube + sign * k + cubes, cubes)
                put(b, i, load(ref, i, 2 + 2 * j), load(ref, i, 3 + 2 * j))
    depth = lines.shape[0]
    for k in range(0, depth, 256):
        turned[:, k : k + 256] = lines[k : k + 256, :].T.astype(jnp.bfloat16)
    fetch.wait()
    for n in range(integrals.shape[1] // LANES):
        out_ref[n * ij : (n + 1) * ij, :] = jnp.dot(
            turned[...],
            integrals[:, n * LANES : (n + 1) * LANES],
            preferred_element_type=jnp.float32,
        )
    used = integrals.shape[1] // LANES * ij
    out_ref[used:, :] = jnp.zeros((out_ref.shape[0] - used, LANES), jnp.float32)


def contract(place, mine, other, integrals, lines_out):
    k, ab = integrals.shape
    ij = mine.shape[-1]
    vmem = pl.BlockSpec(memory_space=pltpu.VMEM)
    return pl.pallas_call(
        contract_kernel,
        out_shape=jax.ShapeDtypeStruct((lines_out, LANES), jnp.float32),
        in_specs=[
            pl.BlockSpec(memory_space=pltpu.SMEM),
            vmem,
            vmem,
            pl.BlockSpec(memory_space=pltpu.HBM),
        ],
        out_specs=vmem,
        scratch_shapes=[
            pltpu.VMEM((k, ab), jnp.bfloat16),
            pltpu.VMEM((k, ij), jnp.float32),
            pltpu.VMEM((ij, k), jnp.bfloat16),
            pltpu.SemaphoreType.DMA,
        ],
        compiler_params=pltpu.CompilerParams(vmem_limit_bytes=32 * MIB),
        cost_estimate=pl.CostEstimate(
            flops=2 * k * ab * ij, bytes_accessed=2 * k * (ab + ij), transcendentals=0
        ),
        name="contract",
    )(place, mine, other, integrals)


def total_kernel(terms_ref, out_ref):
    total = terms_ref[0]
    for r in range(1, terms_ref.shape[0]):
        total = total + terms_ref[r]
    total = total.astype(jnp.bfloat16)
    for r in range(out_ref.shape[0]):
        out_ref[r] = total


def totals(terms):
    vmem = pl.BlockSpec(memory_space=pltpu.VMEM)
    return pl.pallas_call(
        total_kernel,
        out_shape=jax.ShapeDtypeStruct(terms.shape, jnp.bfloat16),
        in_specs=[vmem],
        out_specs=vmem,
        name="totals",
    )(terms)


def order_kernel(lines_ref, out_ref):
    ij, ab = out_ref.shape
    for n in range(ab // LANES):
        out_ref[:, n * LANES : (n + 1) * LANES] = (
            lines_ref[n * ij : (n + 1) * ij, :]
            .astype(jnp.float32)
            .astype(jnp.bfloat16)
        )


def ordered(lines, ij, ab):
    vmem = pl.BlockSpec(memory_space=pltpu.VMEM)
    return pl.pallas_call(
        order_kernel,
        out_shape=jax.ShapeDtypeStruct((ij, ab), jnp.bfloat16),
        in_specs=[vmem],
        out_specs=vmem,
        name="ordered",
    )(lines)


def solution(mesh):
    rows, depth = mesh.shape["row"], mesh.shape["depth"]
    _, inside, _ = depth_groups(depth)

    def shards(integrals, amplitudes):
        ij, ab = amplitudes.shape[1], integrals.shape[1]
        mine = lax.all_gather(
            spread(amplitudes, depth), "depth", axis_index_groups=inside
        )
        other = lax.ppermute(mine, "depth", [(d, d ^ 1) for d in range(depth)])
        here = lax.axis_index("depth")
        place = jnp.stack([here // (CUBE * CORES), lax.rem(here, CORES)])

        share = -(-ij * ab // (LANES * rows * 16)) * 16
        partial = contract(place, mine, other, integrals, rows * share)
        terms = lax.all_to_all(partial.reshape(rows, share, LANES), "row", 0, 0)
        whole = lax.all_to_all(totals(terms), "row", 0, 0)
        return ordered(whole.reshape(rows * share, LANES), ij, ab).T

    placed = (P("row", "depth"), P(("row", "depth"), None))
    return jax.shard_map(
        shards, mesh=mesh, in_specs=placed, out_specs=P("depth", None), check_vma=False
    )
```

```python
import jax
import jax.numpy as jnp
from jax import lax
from jax.experimental import pallas as pl
from jax.experimental.pallas import tpu as pltpu
from jax.sharding import PartitionSpec as P

CUBE = 4
CORES = 2
LANES = 128
MIB = 1 << 20


def depth_groups(depth):
    cubes = depth // (CUBE * CORES)
    inside = [
        [(b * CUBE + i) * CORES + c for i in range(CUBE)]
        for b in range(cubes)
        for c in range(CORES)
    ]
    chips = [[d, d + 1] for d in range(0, depth, CORES)]
    return cubes, inside, chips


def distances(cubes):
    far = list(range(cubes // 2 - 1, 0, -1))
    return far[1:2] + far[:1] + far[2:]


def hop(depth, cubes):
    step = cubes * CUBE * CORES
    return [(d, (d + step * (1 - 2 * (d % CORES))) % depth) for d in range(depth)]


def spread(amplitudes, depth):
    cubes, _, chips = depth_groups(depth)
    pair = lax.all_gather(amplitudes, "depth", axis_index_groups=chips)
    opposite = lax.ppermute(amplitudes, "depth", hop(depth, cubes // 2))
    pairs = [
        lax.ppermute(pair, "depth", hop(depth, k))
        for k in distances(cubes)
    ]
    return jnp.concatenate([amplitudes[None], opposite[None], *pairs], axis=0)


def contract_kernel(
    place_ref, mine_ref, other_ref, integrals_hbm, out_ref, integrals, lines, turned, sem
):
    chips, cubes, rows, ij = mine_ref.shape
    fetch = pltpu.make_async_copy(integrals_hbm, integrals, sem)
    fetch.start()
    cube, core = place_ref[0], place_ref[1]
    first = core == 0
    up = 1 - 2 * core

    def put(b, i, upper, lower):
        at = pl.multiple_of((b * chips + i) * (CORES * rows), 8)
        lines[pl.ds(at, CORES * rows), :] = jnp.concatenate([upper, lower], axis=0)

    def load(ref, i, j):
        return ref[i, j].astype(jnp.float32)

    for i in range(chips):
        for j, away in ((0, 0), (1, cubes // 2)):
            mine, other = load(mine_ref, i, j), load(other_ref, i, j)
            upper, lower = jnp.where(first, mine, other), jnp.where(first, other, mine)
            put(lax.rem(cube + away, cubes), i, upper, lower)
        for j, k in enumerate(distances(cubes)):
            for ref, sign in ((mine_ref, -up), (other_ref, up)):
                b = lax.rem(cube + sign * k + cubes, cubes)
                put(b, i, load(ref, i, 2 + 2 * j), load(ref, i, 3 + 2 * j))
    depth = lines.shape[0]
    for k in range(0, depth, 256):
        turned[:, k : k + 256] = lines[k : k + 256, :].T.astype(jnp.bfloat16)
    fetch.wait()
    for n in range(integrals.shape[1] // LANES):
        out_ref[n * ij : (n + 1) * ij, :] = jnp.dot(
            turned[...],
            integrals[:, n * LANES : (n + 1) * LANES],
            preferred_element_type=jnp.float32,
        )
    used = integrals.shape[1] // LANES * ij
    out_ref[used:, :] = jnp.zeros((out_ref.shape[0] - used, LANES), jnp.float32)


def contract(place, mine, other, integrals, lines_out):
    k, ab = integrals.shape
    ij = mine.shape[-1]
    vmem = pl.BlockSpec(memory_space=pltpu.VMEM)
    return pl.pallas_call(
        contract_kernel,
        out_shape=jax.ShapeDtypeStruct((lines_out, LANES), jnp.float32),
        in_specs=[
            pl.BlockSpec(memory_space=pltpu.SMEM),
            vmem,
            vmem,
            pl.BlockSpec(memory_space=pltpu.HBM),
        ],
        out_specs=vmem,
        scratch_shapes=[
            pltpu.VMEM((k, ab), jnp.bfloat16),
            pltpu.VMEM((k, ij), jnp.float32),
            pltpu.VMEM((ij, k), jnp.bfloat16),
            pltpu.SemaphoreType.DMA,
        ],
        compiler_params=pltpu.CompilerParams(vmem_limit_bytes=32 * MIB),
        cost_estimate=pl.CostEstimate(
            flops=2 * k * ab * ij, bytes_accessed=2 * k * (ab + ij), transcendentals=0
        ),
        name="contract",
    )(place, mine, other, pltpu.with_memory_space_constraint(integrals, pltpu.HBM))


def total_kernel(terms_ref, out_ref):
    total = terms_ref[0]
    for r in range(1, terms_ref.shape[0]):
        total = total + terms_ref[r]
    total = total.astype(jnp.bfloat16)
    for r in range(out_ref.shape[0]):
        out_ref[r] = total


def totals(terms):
    vmem = pl.BlockSpec(memory_space=pltpu.VMEM)
    return pl.pallas_call(
        total_kernel,
        out_shape=jax.ShapeDtypeStruct(terms.shape, jnp.bfloat16),
        in_specs=[vmem],
        out_specs=vmem,
        compiler_params=pltpu.CompilerParams(vmem_limit_bytes=4 * MIB),
        name="totals",
    )(terms)


def order_kernel(lines_ref, out_ref):
    ij, ab = out_ref.shape
    for n in range(ab // LANES):
        out_ref[:, n * LANES : (n + 1) * LANES] = (
            lines_ref[n * ij : (n + 1) * ij, :]
            .astype(jnp.float32)
            .astype(jnp.bfloat16)
        )


def ordered(lines, ij, ab):
    vmem = pl.BlockSpec(memory_space=pltpu.VMEM)
    return pl.pallas_call(
        order_kernel,
        out_shape=jax.ShapeDtypeStruct((ij, ab), jnp.bfloat16),
        in_specs=[vmem],
        out_specs=vmem,
        compiler_params=pltpu.CompilerParams(vmem_limit_bytes=4 * MIB),
        name="ordered",
    )(lines)


def solution(mesh):
    rows, depth = mesh.shape["row"], mesh.shape["depth"]
    _, inside, _ = depth_groups(depth)

    def shards(integrals, amplitudes):
        ij, ab = amplitudes.shape[1], integrals.shape[1]
        mine = lax.all_gather(
            spread(amplitudes, depth), "depth", axis_index_groups=inside
        )
        other = lax.ppermute(mine, "depth", [(d, d ^ 1) for d in range(depth)])
        here = lax.axis_index("depth")
        place = jnp.stack([here // (CUBE * CORES), lax.rem(here, CORES)])

        share = -(-ij * ab // (LANES * rows * 16)) * 16
        partial = contract(place, mine, other, integrals, rows * share)
        terms = lax.all_to_all(partial.reshape(rows, share, LANES), "row", 0, 0)
        whole = lax.all_to_all(totals(terms), "row", 0, 0)
        return ordered(whole.reshape(rows * share, LANES), ij, ab).T

    placed = (P("row", "depth"), P(("row", "depth"), None))
    return jax.shard_map(
        shards, mesh=mesh, in_specs=placed, out_specs=P("depth", None), check_vma=False
    )
```

```python
import jax
import jax.numpy as jnp
from jax import lax
from jax.experimental import pallas as pl
from jax.experimental.pallas import tpu as pltpu
from jax.sharding import PartitionSpec as P

CORES = 2
LANES = 128
MIB = 1 << 20


def contract_kernel(
    core_ref, mine_ref, other_ref, integrals_hbm, out_ref, integrals, lines, turned, sem
):
    chips, rows, ij = mine_ref.shape
    fetch = pltpu.make_async_copy(integrals_hbm, integrals, sem)
    fetch.start()
    first = core_ref[0] == 0
    for z in range(chips):
        mine = mine_ref[z].astype(jnp.float32)
        other = other_ref[z].astype(jnp.float32)
        upper, lower = jnp.where(first, mine, other), jnp.where(first, other, mine)
        at = z * CORES * rows
        lines[at : at + CORES * rows, :] = jnp.concatenate([upper, lower], axis=0)
    depth = lines.shape[0]
    for k in range(0, depth, 256):
        turned[:, k : k + 256] = lines[k : k + 256, :].T.astype(jnp.bfloat16)
    fetch.wait()
    for n in range(integrals.shape[1] // LANES):
        out_ref[n * ij : (n + 1) * ij, :] = jnp.dot(
            turned[...],
            integrals[:, n * LANES : (n + 1) * LANES],
            preferred_element_type=jnp.float32,
        )
    used = integrals.shape[1] // LANES * ij
    out_ref[used:, :] = jnp.zeros((out_ref.shape[0] - used, LANES), jnp.float32)


def contract(core, mine, other, integrals, lines_out):
    k, ab = integrals.shape
    ij = mine.shape[-1]
    vmem = pl.BlockSpec(memory_space=pltpu.VMEM)
    return pl.pallas_call(
        contract_kernel,
        out_shape=jax.ShapeDtypeStruct((lines_out, LANES), jnp.float32),
        in_specs=[
            pl.BlockSpec(memory_space=pltpu.SMEM),
            vmem,
            vmem,
            pl.BlockSpec(memory_space=pltpu.HBM),
        ],
        out_specs=vmem,
        scratch_shapes=[
            pltpu.VMEM((k, ab), jnp.bfloat16),
            pltpu.VMEM((k, ij), jnp.float32),
            pltpu.VMEM((ij, k), jnp.bfloat16),
            pltpu.SemaphoreType.DMA,
        ],
        compiler_params=pltpu.CompilerParams(vmem_limit_bytes=32 * MIB),
        cost_estimate=pl.CostEstimate(
            flops=2 * k * ab * ij, bytes_accessed=2 * k * (ab + ij), transcendentals=0
        ),
        name="contract",
    )(core, mine, other, pltpu.with_memory_space_constraint(integrals, pltpu.HBM))


def total_kernel(terms_ref, out_ref):
    total = terms_ref[0]
    for r in range(1, terms_ref.shape[0]):
        total = total + terms_ref[r]
    total = total.astype(jnp.bfloat16)
    for r in range(out_ref.shape[0]):
        out_ref[r] = total


def totals(terms):
    vmem = pl.BlockSpec(memory_space=pltpu.VMEM)
    return pl.pallas_call(
        total_kernel,
        out_shape=jax.ShapeDtypeStruct(terms.shape, jnp.bfloat16),
        in_specs=[vmem],
        out_specs=vmem,
        compiler_params=pltpu.CompilerParams(vmem_limit_bytes=4 * MIB),
        name="totals",
    )(terms)


def order_kernel(lines_ref, out_ref):
    ij, ab = out_ref.shape
    for n in range(ab // LANES):
        out_ref[:, n * LANES : (n + 1) * LANES] = (
            lines_ref[n * ij : (n + 1) * ij, :]
            .astype(jnp.float32)
            .astype(jnp.bfloat16)
        )


def ordered(lines, ij, ab):
    vmem = pl.BlockSpec(memory_space=pltpu.VMEM)
    return pl.pallas_call(
        order_kernel,
        out_shape=jax.ShapeDtypeStruct((ij, ab), jnp.bfloat16),
        in_specs=[vmem],
        out_specs=vmem,
        compiler_params=pltpu.CompilerParams(vmem_limit_bytes=4 * MIB),
        name="ordered",
    )(lines)


def solution(mesh):
    rows, depth = mesh.shape["row"], mesh.shape["depth"]
    columns = [list(range(c, depth, CORES)) for c in range(CORES)]
    swap = [(d, d ^ 1) for d in range(depth)]

    def shards(integrals, amplitudes):
        ij, ab = amplitudes.shape[1], integrals.shape[1]
        mine = lax.all_gather(amplitudes, "depth", axis_index_groups=columns)
        other = lax.ppermute(mine, "depth", swap)
        core = lax.rem(lax.axis_index("depth"), CORES).reshape(1)

        share = -(-ij * ab // (LANES * rows * 16)) * 16
        partial = contract(core, mine, other, integrals, rows * share)
        terms = lax.all_to_all(partial.reshape(rows, share, LANES), "row", 0, 0)
        whole = lax.all_to_all(totals(terms), "row", 0, 0)
        return ordered(whole.reshape(rows * share, LANES), ij, ab).T

    placed = (P("row", "depth"), P(("row", "depth"), None))
    return jax.shard_map(
        shards, mesh=mesh, in_specs=placed, out_specs=P("depth", None), check_vma=False
    )
```

```python
import jax
import jax.numpy as jnp
from jax import lax
from jax.experimental import pallas as pl
from jax.experimental.pallas import tpu as pltpu
from jax.sharding import PartitionSpec as P

CORES = 2
LANES = 128
MIB = 1 << 20


def contract_kernel(
    ring_ref, mine_ref, other_ref, integrals_hbm, out_ref, integrals, lines, turned, sem
):
    chips, rows, ij = mine_ref.shape
    fetch = pltpu.make_async_copy(integrals_hbm, integrals, sem)
    fetch.start()
    even = ring_ref[0] == 0
    for z in range(chips):
        mine = mine_ref[z].astype(jnp.float32)
        other = other_ref[z].astype(jnp.float32)
        first = even if z % 2 == 0 else jnp.logical_not(even)
        upper, lower = jnp.where(first, mine, other), jnp.where(first, other, mine)
        at = z * CORES * rows
        lines[at : at + CORES * rows, :] = jnp.concatenate([upper, lower], axis=0)
    depth = lines.shape[0]
    for k in range(0, depth, 256):
        turned[:, k : k + 256] = lines[k : k + 256, :].T.astype(jnp.bfloat16)
    fetch.wait()
    ab = integrals.shape[1]
    for n in range(0, ab, 2 * LANES):
        end = min(n + 2 * LANES, ab)
        block = jnp.dot(
            turned[...], integrals[:, n:end], preferred_element_type=jnp.float32
        )
        for m in range(n, end, LANES):
            at = m // LANES * ij
            out_ref[at : at + ij, :] = block[:, m - n : m - n + LANES]
    used = ab // LANES * ij
    out_ref[used:, :] = jnp.zeros((out_ref.shape[0] - used, LANES), jnp.float32)


def contract(ring, mine, other, integrals, lines_out):
    k, ab = integrals.shape
    ij = mine.shape[-1]
    vmem = pl.BlockSpec(memory_space=pltpu.VMEM)
    return pl.pallas_call(
        contract_kernel,
        out_shape=jax.ShapeDtypeStruct((lines_out, LANES), jnp.float32),
        in_specs=[
            pl.BlockSpec(memory_space=pltpu.SMEM),
            vmem,
            vmem,
            pl.BlockSpec(memory_space=pltpu.HBM),
        ],
        out_specs=vmem,
        scratch_shapes=[
            pltpu.VMEM((k, ab), jnp.bfloat16),
            pltpu.VMEM((k, ij), jnp.float32),
            pltpu.VMEM((ij, k), jnp.bfloat16),
            pltpu.SemaphoreType.DMA,
        ],
        compiler_params=pltpu.CompilerParams(vmem_limit_bytes=32 * MIB),
        cost_estimate=pl.CostEstimate(
            flops=2 * k * ab * ij, bytes_accessed=2 * k * (ab + ij), transcendentals=0
        ),
        name="contract",
    )(ring, mine, other, pltpu.with_memory_space_constraint(integrals, pltpu.HBM))


def total_kernel(terms_ref, out_ref):
    total = terms_ref[0]
    for r in range(1, terms_ref.shape[0]):
        total = total + terms_ref[r]
    total = total.astype(jnp.bfloat16)
    for r in range(out_ref.shape[0]):
        out_ref[r] = total


def totals(terms):
    vmem = pl.BlockSpec(memory_space=pltpu.VMEM)
    return pl.pallas_call(
        total_kernel,
        out_shape=jax.ShapeDtypeStruct(terms.shape, jnp.bfloat16),
        in_specs=[vmem],
        out_specs=vmem,
        compiler_params=pltpu.CompilerParams(vmem_limit_bytes=4 * MIB),
        name="totals",
    )(terms)


def order_kernel(lines_ref, out_ref):
    ij, ab = out_ref.shape
    for n in range(ab // LANES):
        out_ref[:, n * LANES : (n + 1) * LANES] = (
            lines_ref[n * ij : (n + 1) * ij, :]
            .astype(jnp.float32)
            .astype(jnp.bfloat16)
        )


def ordered(lines, ij, ab):
    vmem = pl.BlockSpec(memory_space=pltpu.VMEM)
    return pl.pallas_call(
        order_kernel,
        out_shape=jax.ShapeDtypeStruct((ij, ab), jnp.bfloat16),
        in_specs=[vmem],
        out_specs=vmem,
        compiler_params=pltpu.CompilerParams(vmem_limit_bytes=4 * MIB),
        name="ordered",
    )(lines)


def solution(mesh):
    rows, depth = mesh.shape["row"], mesh.shape["depth"]
    rings = [
        [z * CORES + (q + z) % CORES for z in range(depth // CORES)]
        for q in range(CORES)
    ]
    swap = [(d, d ^ 1) for d in range(depth)]

    def shards(integrals, amplitudes):
        ij, ab = amplitudes.shape[1], integrals.shape[1]
        mine = lax.all_gather(amplitudes, "depth", axis_index_groups=rings)
        other = lax.ppermute(mine, "depth", swap)
        here = lax.axis_index("depth")
        ring = lax.rem(here // CORES + here, CORES).reshape(1)

        share = -(-ij * ab // (LANES * rows * 16)) * 16
        partial = contract(ring, mine, other, integrals, rows * share)
        terms = lax.all_to_all(partial.reshape(rows, share, LANES), "row", 0, 0)
        whole = lax.all_to_all(totals(terms), "row", 0, 0)
        return ordered(whole.reshape(rows * share, LANES), ij, ab).T

    placed = (P("row", "depth"), P(("row", "depth"), None))
    return jax.shard_map(
        shards, mesh=mesh, in_specs=placed, out_specs=P("depth", None), check_vma=False
    )
```

```python
import jax
import jax.numpy as jnp
from jax import lax
from jax.experimental import pallas as pl
from jax.experimental.pallas import tpu as pltpu
from jax.sharding import PartitionSpec as P

CORES = 2
LANES = 128
MIB = 1 << 20


def contract_kernel(
    ring_ref, mine_ref, other_ref, integrals_hbm, out_ref, integrals, lines, turned, sem
):
    chips, rows, ij = mine_ref.shape
    fetch = pltpu.make_async_copy(integrals_hbm, integrals, sem)
    fetch.start()
    even = ring_ref[0] == 0
    for member in range(chips):
        z = (member + chips // 2) % chips
        mine = mine_ref[member].astype(jnp.float32)
        other = other_ref[member].astype(jnp.float32)
        first = even if z % 2 == 0 else jnp.logical_not(even)
        upper, lower = jnp.where(first, mine, other), jnp.where(first, other, mine)
        at = z * CORES * rows
        lines[at : at + CORES * rows, :] = jnp.concatenate([upper, lower], axis=0)
    depth = lines.shape[0]
    for k in range(0, depth, 256):
        turned[:, k : k + 256] = lines[k : k + 256, :].T.astype(jnp.bfloat16)
    fetch.wait()
    ab = integrals.shape[1]
    for n in range(0, ab, 2 * LANES):
        end = min(n + 2 * LANES, ab)
        block = jnp.dot(
            turned[...], integrals[:, n:end], preferred_element_type=jnp.float32
        )
        for m in range(n, end, LANES):
            at = m // LANES * ij
            out_ref[at : at + ij, :] = block[:, m - n : m - n + LANES]
    used = ab // LANES * ij
    out_ref[used:, :] = jnp.zeros((out_ref.shape[0] - used, LANES), jnp.float32)


def contract(ring, mine, other, integrals, lines_out):
    k, ab = integrals.shape
    ij = mine.shape[-1]
    vmem = pl.BlockSpec(memory_space=pltpu.VMEM)
    return pl.pallas_call(
        contract_kernel,
        out_shape=jax.ShapeDtypeStruct((lines_out, LANES), jnp.float32),
        in_specs=[
            pl.BlockSpec(memory_space=pltpu.SMEM),
            vmem,
            vmem,
            pl.BlockSpec(memory_space=pltpu.HBM),
        ],
        out_specs=vmem,
        scratch_shapes=[
            pltpu.VMEM((k, ab), jnp.bfloat16),
            pltpu.VMEM((k, ij), jnp.float32),
            pltpu.VMEM((ij, k), jnp.bfloat16),
            pltpu.SemaphoreType.DMA,
        ],
        compiler_params=pltpu.CompilerParams(vmem_limit_bytes=32 * MIB),
        cost_estimate=pl.CostEstimate(
            flops=2 * k * ab * ij, bytes_accessed=2 * k * (ab + ij), transcendentals=0
        ),
        name="contract",
    )(ring, mine, other, pltpu.with_memory_space_constraint(integrals, pltpu.HBM))


def total_kernel(terms_ref, out_ref):
    total = terms_ref[0]
    for r in range(1, terms_ref.shape[0]):
        total = total + terms_ref[r]
    total = total.astype(jnp.bfloat16)
    for r in range(out_ref.shape[0]):
        out_ref[r] = total


def totals(terms):
    vmem = pl.BlockSpec(memory_space=pltpu.VMEM)
    return pl.pallas_call(
        total_kernel,
        out_shape=jax.ShapeDtypeStruct(terms.shape, jnp.bfloat16),
        in_specs=[vmem],
        out_specs=vmem,
        compiler_params=pltpu.CompilerParams(vmem_limit_bytes=4 * MIB),
        name="totals",
    )(terms)


def order_kernel(lines_ref, out_ref):
    ij, ab = out_ref.shape
    for n in range(ab // LANES):
        out_ref[:, n * LANES : (n + 1) * LANES] = (
            lines_ref[n * ij : (n + 1) * ij, :]
            .astype(jnp.float32)
            .astype(jnp.bfloat16)
        )


def ordered(lines, ij, ab):
    vmem = pl.BlockSpec(memory_space=pltpu.VMEM)
    return pl.pallas_call(
        order_kernel,
        out_shape=jax.ShapeDtypeStruct((ij, ab), jnp.bfloat16),
        in_specs=[vmem],
        out_specs=vmem,
        compiler_params=pltpu.CompilerParams(vmem_limit_bytes=4 * MIB),
        name="ordered",
    )(lines)


def solution(mesh):
    rows, depth = mesh.shape["row"], mesh.shape["depth"]
    chips = depth // CORES
    order = [(member + chips // 2) % chips for member in range(chips)]
    rings = [[z * CORES + (q + z) % CORES for z in order] for q in range(CORES)]
    swap = [(d, d ^ 1) for d in range(depth)]

    def shards(integrals, amplitudes):
        ij, ab = amplitudes.shape[1], integrals.shape[1]
        mine = lax.all_gather(amplitudes, "depth", axis_index_groups=rings)
        other = lax.ppermute(mine, "depth", swap)
        here = lax.axis_index("depth")
        ring = lax.rem(here // CORES + here, CORES).reshape(1)

        share = -(-ij * ab // (LANES * rows * 16)) * 16
        partial = contract(ring, mine, other, integrals, rows * share)
        terms = lax.all_to_all(partial.reshape(rows, share, LANES), "row", 0, 0)
        whole = lax.all_to_all(totals(terms), "row", 0, 0)
        return ordered(whole.reshape(rows * share, LANES), ij, ab).T

    placed = (P("row", "depth"), P(("row", "depth"), None))
    return jax.shard_map(
        shards, mesh=mesh, in_specs=placed, out_specs=P("depth", None), check_vma=False
    )
```

```python
import jax
import jax.numpy as jnp
from jax import lax
from jax.experimental import pallas as pl
from jax.experimental.pallas import tpu as pltpu
from jax.sharding import PartitionSpec as P

CORES = 2
LANES = 128
MIB = 1 << 20


def contract_kernel(
    ring_ref, mine_ref, other_ref, integrals_hbm, out_ref, integrals, lines, turned, sem
):
    chips, rows, ij = mine_ref.shape
    fetch = pltpu.make_async_copy(integrals_hbm, integrals, sem)
    fetch.start()
    members, share, _ = out_ref.shape

    def put(line, values):
        done = 0
        while done < values.shape[0]:
            owner, at = divmod(line + done, share)
            size = min(share - at, values.shape[0] - done)
            slot = members - 1 - owner
            out_ref[slot, at : at + size, :] = values[done : done + size]
            done += size

    even = ring_ref[0] == 0
    for z in range(chips):
        mine = mine_ref[z].astype(jnp.float32)
        other = other_ref[z].astype(jnp.float32)
        first = even if z % 2 == 0 else jnp.logical_not(even)
        upper, lower = jnp.where(first, mine, other), jnp.where(first, other, mine)
        at = z * CORES * rows
        lines[at : at + CORES * rows, :] = jnp.concatenate([upper, lower], axis=0)
    depth = lines.shape[0]
    for k in range(0, depth, 256):
        turned[:, k : k + 256] = lines[k : k + 256, :].T.astype(jnp.bfloat16)
    fetch.wait()
    ab = integrals.shape[1]
    for n in range(0, ab, 2 * LANES):
        end = min(n + 2 * LANES, ab)
        block = jnp.dot(
            turned[...], integrals[:, n:end], preferred_element_type=jnp.float32
        )
        for m in range(n, end, LANES):
            first_line = m // LANES * ij
            put(first_line, block[:, m - n : m - n + LANES])
    used = ab // LANES * ij
    put(used, jnp.zeros((members * share - used, LANES), jnp.float32))


def contract(ring, mine, other, integrals, rows, share):
    k, ab = integrals.shape
    ij = mine.shape[-1]
    vmem = pl.BlockSpec(memory_space=pltpu.VMEM)
    return pl.pallas_call(
        contract_kernel,
        out_shape=jax.ShapeDtypeStruct((rows, share, LANES), jnp.float32),
        in_specs=[
            pl.BlockSpec(memory_space=pltpu.SMEM),
            vmem,
            vmem,
            pl.BlockSpec(memory_space=pltpu.HBM),
        ],
        out_specs=vmem,
        scratch_shapes=[
            pltpu.VMEM((k, ab), jnp.bfloat16),
            pltpu.VMEM((k, ij), jnp.float32),
            pltpu.VMEM((ij, k), jnp.bfloat16),
            pltpu.SemaphoreType.DMA,
        ],
        compiler_params=pltpu.CompilerParams(vmem_limit_bytes=32 * MIB),
        cost_estimate=pl.CostEstimate(
            flops=2 * k * ab * ij, bytes_accessed=2 * k * (ab + ij), transcendentals=0
        ),
        name="contract",
    )(ring, mine, other, pltpu.with_memory_space_constraint(integrals, pltpu.HBM))


def total_kernel(terms_ref, out_ref):
    total = terms_ref[0]
    for r in range(1, terms_ref.shape[0]):
        total = total + terms_ref[r]
    total = total.astype(jnp.bfloat16)
    for r in range(out_ref.shape[0]):
        out_ref[r] = total


def totals(terms):
    vmem = pl.BlockSpec(memory_space=pltpu.VMEM)
    return pl.pallas_call(
        total_kernel,
        out_shape=jax.ShapeDtypeStruct(terms.shape, jnp.bfloat16),
        in_specs=[vmem],
        out_specs=vmem,
        compiler_params=pltpu.CompilerParams(vmem_limit_bytes=4 * MIB),
        name="totals",
    )(terms)


def order_kernel(lines_ref, out_ref):
    ij, ab = out_ref.shape
    for n in range(ab // LANES):
        out_ref[:, n * LANES : (n + 1) * LANES] = (
            lines_ref[n * ij : (n + 1) * ij, :]
            .astype(jnp.float32)
            .astype(jnp.bfloat16)
        )


def ordered(lines, ij, ab):
    vmem = pl.BlockSpec(memory_space=pltpu.VMEM)
    return pl.pallas_call(
        order_kernel,
        out_shape=jax.ShapeDtypeStruct((ij, ab), jnp.bfloat16),
        in_specs=[vmem],
        out_specs=vmem,
        compiler_params=pltpu.CompilerParams(vmem_limit_bytes=4 * MIB),
        name="ordered",
    )(lines)


def solution(mesh):
    rows, depth = mesh.shape["row"], mesh.shape["depth"]
    rings = [
        [z * CORES + (q + z) % CORES for z in range(depth // CORES)]
        for q in range(CORES)
    ]
    swap = [(d, d ^ 1) for d in range(depth)]
    turned = [list(range(rows))[::-1]]

    def shards(integrals, amplitudes):
        ij, ab = amplitudes.shape[1], integrals.shape[1]
        mine = lax.all_gather(amplitudes, "depth", axis_index_groups=rings)
        other = lax.ppermute(mine, "depth", swap)
        here = lax.axis_index("depth")
        ring = lax.rem(here // CORES + here, CORES).reshape(1)

        share = -(-ij * ab // (LANES * rows * 16)) * 16
        partial = contract(ring, mine, other, integrals, rows, share)
        terms = lax.all_to_all(partial, "row", 0, 0, axis_index_groups=turned)
        whole = lax.all_to_all(totals(terms), "row", 0, 0)
        return ordered(whole.reshape(rows * share, LANES), ij, ab).T

    placed = (P("row", "depth"), P(("row", "depth"), None))
    return jax.shard_map(
        shards, mesh=mesh, in_specs=placed, out_specs=P("depth", None), check_vma=False
    )
```

```python
import jax
import jax.numpy as jnp
from jax import lax
from jax.experimental import pallas as pl
from jax.experimental.pallas import tpu as pltpu
from jax.sharding import PartitionSpec as P

CORES = 2
LANES = 128
MIB = 1 << 20


def contract_kernel(
    ring_ref, mine_ref, other_ref, integrals_hbm, out_ref, integrals, lines, turned, sem
):
    chips, rows, ij = mine_ref.shape
    fetch = pltpu.make_async_copy(integrals_hbm, integrals, sem)
    fetch.start()
    members, share, _ = out_ref.shape

    def put(line, values):
        done = 0
        while done < values.shape[0]:
            owner, at = divmod(line + done, share)
            size = min(share - at, values.shape[0] - done)
            out_ref[owner, at : at + size, :] = values[done : done + size]
            done += size

    even = ring_ref[0] == 0
    for z in range(chips):
        mine = mine_ref[z].astype(jnp.float32)
        other = other_ref[z].astype(jnp.float32)
        first = even if z % 2 == 0 else jnp.logical_not(even)
        upper, lower = jnp.where(first, mine, other), jnp.where(first, other, mine)
        at = z * CORES * rows
        lines[at : at + CORES * rows, :] = jnp.concatenate([upper, lower], axis=0)
    depth = lines.shape[0]
    for k in range(0, depth, 256):
        turned[:, k : k + 256] = lines[k : k + 256, :].T.astype(jnp.bfloat16)
    fetch.wait()
    ab = integrals.shape[1]
    for n in range(0, ab, 2 * LANES):
        end = min(n + 2 * LANES, ab)
        block = jnp.dot(
            turned[...], integrals[:, n:end], preferred_element_type=jnp.float32
        )
        for m in range(n, end, LANES):
            first_line = m // LANES * ij
            put(first_line, block[:, m - n : m - n + LANES])
    used = ab // LANES * ij
    put(used, jnp.zeros((members * share - used, LANES), jnp.float32))


def contract(ring, mine, other, integrals, rows, share):
    k, ab = integrals.shape
    ij = mine.shape[-1]
    vmem = pl.BlockSpec(memory_space=pltpu.VMEM)
    return pl.pallas_call(
        contract_kernel,
        out_shape=jax.ShapeDtypeStruct((rows, share, LANES), jnp.float32),
        in_specs=[
            pl.BlockSpec(memory_space=pltpu.SMEM),
            vmem,
            vmem,
            pl.BlockSpec(memory_space=pltpu.HBM),
        ],
        out_specs=vmem,
        scratch_shapes=[
            pltpu.VMEM((k, ab), jnp.bfloat16),
            pltpu.VMEM((k, ij), jnp.float32),
            pltpu.VMEM((ij, k), jnp.bfloat16),
            pltpu.SemaphoreType.DMA,
        ],
        compiler_params=pltpu.CompilerParams(vmem_limit_bytes=32 * MIB),
        cost_estimate=pl.CostEstimate(
            flops=2 * k * ab * ij, bytes_accessed=2 * k * (ab + ij), transcendentals=0
        ),
        name="contract",
    )(ring, mine, other, pltpu.with_memory_space_constraint(integrals, pltpu.HBM))


def total_kernel(terms_ref, out_ref):
    total = terms_ref[0]
    for r in range(1, terms_ref.shape[0]):
        total = total + terms_ref[r]
    total = total.astype(jnp.bfloat16)
    for r in range(out_ref.shape[0]):
        out_ref[r] = total


def totals(terms):
    vmem = pl.BlockSpec(memory_space=pltpu.VMEM)
    return pl.pallas_call(
        total_kernel,
        out_shape=jax.ShapeDtypeStruct(terms.shape, jnp.bfloat16),
        in_specs=[vmem],
        out_specs=vmem,
        compiler_params=pltpu.CompilerParams(vmem_limit_bytes=4 * MIB),
        name="totals",
    )(terms)


def order_kernel(lines_ref, out_ref):
    ij, ab = out_ref.shape
    for n in range(ab // LANES):
        out_ref[:, n * LANES : (n + 1) * LANES] = (
            lines_ref[n * ij : (n + 1) * ij, :]
            .astype(jnp.float32)
            .astype(jnp.bfloat16)
        )


def ordered(lines, ij, ab):
    vmem = pl.BlockSpec(memory_space=pltpu.VMEM)
    return pl.pallas_call(
        order_kernel,
        out_shape=jax.ShapeDtypeStruct((ij, ab), jnp.bfloat16),
        in_specs=[vmem],
        out_specs=vmem,
        compiler_params=pltpu.CompilerParams(vmem_limit_bytes=4 * MIB),
        name="ordered",
    )(lines)


def solution(mesh):
    rows, depth = mesh.shape["row"], mesh.shape["depth"]
    rings = [
        [z * CORES + (q + z) % CORES for z in range(depth // CORES)]
        for q in range(CORES)
    ]
    swap = [(d, d ^ 1) for d in range(depth)]
    turned = [list(range(rows))[::-1]]

    def shards(integrals, amplitudes):
        ij, ab = amplitudes.shape[1], integrals.shape[1]
        mine = lax.all_gather(amplitudes, "depth", axis_index_groups=rings)
        other = lax.ppermute(mine, "depth", swap)
        here = lax.axis_index("depth")
        ring = lax.rem(here // CORES + here, CORES).reshape(1)

        share = -(-ij * ab // (LANES * rows * 16)) * 16
        partial = contract(ring, mine, other, integrals, rows, share)
        terms = lax.all_to_all(partial, "row", 0, 0, axis_index_groups=turned)
        whole = lax.all_to_all(
            totals(terms), "row", 0, 0, axis_index_groups=turned
        )
        return ordered(whole.reshape(rows * share, LANES), ij, ab).T

    placed = (P("row", "depth"), P(("row", "depth"), None))
    return jax.shard_map(
        shards, mesh=mesh, in_specs=placed, out_specs=P("depth", None), check_vma=False
    )
```
